32 devices in a mesh: replica: 16 (over z, x, core), shard: 2 (over y).
Axes of the slice: x: 2, y: 2, z: 4, core: 2. Of those that a mesh axis runs over, the one named last changes fastest.
Arguments:
- normed: bfloat16 [8192, 8192], P(('replica', 'shard')), may hold values from -96 to 96
- out_grads: bfloat16 [8192, 1024], P(('replica', 'shard')), may hold values from -4 to 4
- weight: float32 [8192, 1024], P(('replica', 'shard')), may hold values from -6 to 6
- moment: float32 [8192, 1024], P(('replica', 'shard')), may hold values from -6 to 6
- variance: float32 [8192, 1024], P(('replica', 'shard')), may hold values from 0.5 to 8
Outputs:
- new_weight: float32 [8192, 1024], P(('replica', 'shard'))
- new_moment: float32 [8192, 1024], P(('replica', 'shard'))
- new_variance: float32 [8192, 1024], P(('replica', 'shard'))
The draws below stay inside these ranges and needn't reach their ends.
All inputs are finite; a program needn't handle non-finite values.
Results may differ from the reference program's by a relative error of at most 0.002.
Values may be sent and summed in bfloat16 or wider, within the bound.
No kernel may reach another device: no remote copies, remote signals or barrier semaphores. Data moves between devices by JAX's collectives and lax.ppermute only.
A program may use at most 128 MiB of HBM per device.

```python
import math
import jax
import jax.numpy as jnp
from jax import lax

D = 8192
TOK_DEV = 256
STEP = 10
C = 1024
TOKENS = 8192
N_REPLICA = 16
N_SHARD = 2


def draw_normed(key, part):
    key_base = jax.random.fold_in(jax.random.fold_in(key, 11), 0)
    key_scale = jax.random.fold_in(jax.random.fold_in(key, 11), 1)
    key_pair = jax.random.fold_in(jax.random.fold_in(key, 11), 3)
    spread = jax.random.uniform(key_scale, (D,), jnp.float32)
    ramp = 1.0 + 2.0 * jnp.arange(D, dtype=jnp.float32) / (D - 1)
    scale = ramp * jnp.exp(spread * math.log(10.0)) / 10.0
    blocks = TOKENS // TOK_DEV
    width = D // blocks
    pairing = jax.random.permutation(key_pair, blocks)
    tok_block = jnp.arange(TOKENS, dtype=jnp.int32) // TOK_DEV
    col_block = jnp.arange(D, dtype=jnp.int32) // width
    paired = pairing[tok_block][:, None] == col_block[None, :]
    factor = jnp.where(paired, jnp.float32(8.0), jnp.float32(1.0))
    base = jnp.clip(jax.random.normal(key_base, (TOKENS, D), jnp.float32), -4.0, 4.0)
    return (base * scale[None, :] * factor).astype(jnp.bfloat16)


def draw_out_grads(key, part):
    key_base, key_scale = jax.random.split(jax.random.fold_in(key, 12), 2)
    spread = jax.random.uniform(key_scale, (C,), jnp.float32)
    scale = jnp.exp(spread * math.log(10.0)) / 10.0
    base = jnp.clip(jax.random.normal(key_base, (TOKENS, C), jnp.float32), -4.0, 4.0)
    return (base * scale[None, :]).astype(jnp.bfloat16)


def shard_levels(rng, extent, pieces, low, top_value):
    level, own = 1.0, jax.random.fold_in(rng, 6)
    for dim, shards_of in pieces:
        draws = jnp.exp(jax.random.uniform(jax.random.fold_in(own, dim), (shards_of,), jnp.float32, low / len(pieces), top_value / len(pieces)))
        level = level * jnp.repeat(draws, extent[dim] // shards_of).reshape([-1 if axis == dim else 1 for axis in range(len(extent))])
    return level


def bell_draw(key, extent, deviation, most, cuts=(), kind=jnp.bfloat16):
    values = jax.random.normal(key, extent, jnp.float32) * deviation
    if len(cuts) > 0:
        values = shard_levels(key, extent, cuts, -0.22, 0.18) * values
    return jnp.clip(values, min=-most, max=most).astype(kind)


def setup_inputs(seed: int = 0) -> dict:
    key_of = jax.random.split(jax.random.key(seed), 6)
    return {
        "normed": draw_normed(jax.random.fold_in(key_of[5], 71), 0),
        "out_grads": draw_out_grads(jax.random.fold_in(key_of[5], 71), 0),
        "weight": bell_draw(key_of[2], (D, C), 1.0, 6.0, ((0, 32),), jnp.float32),
        "moment": bell_draw(key_of[3], (D, C), 1.0, 6.0, ((0, 32),), jnp.float32),
        "variance": jnp.clip(jnp.exp(math.log(8.0) - 2.7725887 * jax.random.uniform(key_of[4], (D, C), jnp.float32) ** shard_levels(key_of[4], (D, C), ((0, 32),), -0.2, 0.2)), 0.5, 8.0),
    }


def reference(normed, out_grads, weight, moment, variance):
    blocks = N_REPLICA * N_SHARD
    inputs = normed.reshape(blocks, TOK_DEV, D)
    grads = out_grads.reshape(blocks, TOK_DEV, C)

    def accumulate(total, pair):
        left = pair[0].astype(jnp.float32)
        right = pair[1].astype(jnp.float32)
        part = jnp.dot(left.T, right, precision=lax.Precision.HIGHEST, preferred_element_type=jnp.float32)
        part = lax.optimization_barrier(part.astype(jnp.bfloat16)).astype(jnp.float32)
        return (total + part, None)
    grad, unused = lax.scan(accumulate, jnp.zeros((D, C), jnp.float32), (inputs, grads))
    squares = jnp.sum(grad * grad)
    limit = jnp.sqrt(jnp.float32(D * C))
    clip = jnp.minimum(jnp.float32(1.0), limit / (jnp.sqrt(squares) + 1e-06))
    scaled = clip * grad
    new_moment = 0.9 * moment + 0.1 * scaled
    new_variance = 0.95 * variance + 0.05 * scaled * scaled
    first = new_moment / (1.0 - 0.9 ** STEP)
    second = new_variance / (1.0 - 0.95 ** STEP)
    new_weight = weight - 0.01 * (first / (jnp.sqrt(second) + 1e-08) + 0.1 * weight)
    return (new_weight, new_moment, new_variance)
```

```python
import functools
import jax
import jax.numpy as jnp
from jax import lax
from jax.experimental import pallas as pl
from jax.experimental.pallas import tpu as pltpu
from jax.sharding import PartitionSpec as P

STEP = 10
AXES = ("replica", "shard")
F32 = jnp.float32
BF16 = jnp.bfloat16
VMEM_LIMIT = 32 * 2**20


def flip(values, n_replica, n_shard, replica_bits, shard_bits):
    pairs = []
    for rep in range(n_replica):
        for sh in range(n_shard):
            there = (rep ^ replica_bits) * n_shard + (sh ^ shard_bits)
            pairs.append((rep * n_shard + sh, there))
    return lax.ppermute(values, AXES, pairs)


def pack_kernel(chunks, n_shard, own, where, normed, *refs):
    outs, (buf, turned, sems) = refs[: 2 + 4 * chunks], refs[2 + 4 * chunks :]
    mine, core, cross = outs[0], outs[1], outs[2:]
    rest, x, c, y = where[0], where[1], where[2], where[3]
    width = n_shard * own
    order = []
    for step in range(chunks):
        for dx, dc in ((1, 0), (1, 1)):
            order.append((step, dx, dc))
    for step in range(chunks):
        for dx, dc in ((0, 1), (0, 0)):
            order.append((step, dx, dc))
    copies = []
    for at, (step, dx, dc) in enumerate(order):
        k = chunks - 1 - step
        block = ((rest ^ k) * 2 + (x ^ dx)) * 2 + (c ^ dc)
        start = pl.multiple_of(block * width, width)
        copy = pltpu.make_async_copy(normed.at[:, pl.ds(start, width)], buf.at[at], sems.at[at])
        copy.start()
        copies.append(copy)
    for at, (step, dx, dc) in enumerate(order):
        copies[at].wait()
        turned[...] = buf[at].T
        for j in range(n_shard):
            rows = turned[pl.ds(pl.multiple_of((y ^ j) * own, own), own), :]
            if dx:
                base = 4 * step + 2 * dc
                if j == 0:
                    cross[base + 1][...] = rows
                else:
                    cross[base][pl.ds((j - 1) * own, own), :] = rows
            else:
                into = core if dc else mine
                into[pl.ds(step * width + j * own, own), :] = rows


def product_kernel(rounds, a0, a1, a2, a3, b0, b1, b2, b3, out):
    lhs = (a0, a1, a2, a3)
    rhs = (b0, b1, b2, b3)
    tile = 256
    for col in range(0, out.shape[1], tile):
        total = None
        for a, b in zip(lhs, rhs):
            part = jnp.dot(a[...], b[:, pl.ds(col, tile)], preferred_element_type=F32)
            part = part.astype(BF16).astype(F32)
            total = part if total is None else total + part
        out[:, pl.ds(col, tile)] = total.astype(out.dtype)


def product(lhs, rhs, dtype):
    rows, columns = lhs[0].shape[0], rhs[0].shape[1]
    depth = rhs[0].shape[0]
    return pl.pallas_call(
        functools.partial(product_kernel, 4),
        out_shape=jax.ShapeDtypeStruct((rows, columns), dtype),
        in_specs=[pl.BlockSpec(memory_space=pltpu.VMEM)] * 8,
        out_specs=pl.BlockSpec(memory_space=pltpu.VMEM),
        compiler_params=pltpu.CompilerParams(vmem_limit_bytes=VMEM_LIMIT),
        cost_estimate=pl.CostEstimate(
            flops=8 * rows * columns * depth,
            bytes_accessed=4 * (rows + columns) * depth * 2 + rows * columns * 4,
            transcendentals=0,
        ),
    )(*lhs, *rhs)


def shards(normed, out_grads, weight, moment, variance):
    depth, width = normed.shape
    columns = out_grads.shape[1]
    n_replica = lax.axis_size("replica")
    n_shard = lax.axis_size("shard")
    chunks = n_replica // 4
    own = width // (n_replica * n_shard)
    group = n_shard * own
    rep = lax.axis_index("replica")
    where = jnp.stack([rep // 4, (rep // 2) % 2, rep % 2, lax.axis_index("shard")]).astype(jnp.int32)
    move = lambda values, rb, sb: flip(values, n_replica, n_shard, rb, sb)

    b_own = out_grads
    b_x = move(b_own, 2, 0)
    b_core = move(b_own, 1, 0)

    shapes = [jax.ShapeDtypeStruct((chunks * group, depth), BF16)] * 2
    for _ in range(chunks):
        for _ in range(2):
            shapes.append(jax.ShapeDtypeStruct((group - own, depth), BF16))
            shapes.append(jax.ShapeDtypeStruct((own, depth), BF16))
    packed = pl.pallas_call(
        functools.partial(pack_kernel, chunks, n_shard, own),
        out_shape=shapes,
        in_specs=[pl.BlockSpec(memory_space=pltpu.SMEM), pl.BlockSpec(memory_space=pl.ANY)],
        out_specs=[pl.BlockSpec(memory_space=pltpu.VMEM)] * len(shapes),
        scratch_shapes=[
            pltpu.VMEM((4 * chunks, depth, group), BF16),
            pltpu.VMEM((group, depth), BF16),
            pltpu.SemaphoreType.DMA((4 * chunks,)),
        ],
        compiler_params=pltpu.CompilerParams(vmem_limit_bytes=VMEM_LIMIT),
        cost_estimate=pl.CostEstimate(flops=0, bytes_accessed=4 * width * depth, transcendentals=0),
    )(where, normed)
    a_own, cross = packed[0], packed[2:]

    b_xc = None
    a_core = move(packed[1], 1, 0)
    far, near = [None] * chunks, [None] * chunks
    order = [("far", 0)]
    for step in range(1, chunks):
        order += [("far", step), ("near", step - 1)]
    order.append(("near", chunks - 1))
    for kind, step in order:
        base = 4 * step + (0 if kind == "far" else 1)
        got = (move(cross[base], 2, 0), move(cross[base + 2], 3, 0))
        (far if kind == "far" else near)[step] = got
    b_xc = move(b_x, 1, 0)
    rhs = (b_own, b_core, b_x, b_xc)

    def rows_of(values, step, first, count):
        start = step * group + first
        return lax.slice_in_dim(values, start, start + count, axis=0)

    sums = [None] * chunks
    arriving = [[] for _ in range(chunks)]
    for step in range(chunks):
        k = chunks - 1 - step
        lhs = [rows_of(a_own, step, own, group - own), rows_of(a_core, step, own, group - own), *far[step]]
        outward = product(lhs, rhs, BF16)
        lhs = [rows_of(a_own, step, 0, own), rows_of(a_core, step, 0, own), *near[step]]
        total = product(lhs, rhs, F32)
        for j in range(1, n_shard):
            piece = lax.slice_in_dim(outward, (j - 1) * own, j * own, axis=0)
            total = total + move(piece, 0, j).astype(F32)
        for piece in arriving[k]:
            total = total + piece.astype(F32)
        if k > 0:
            low = k & -k
            arriving[k ^ low].append(move(total.astype(BF16), 4 * low, 0))
        sums[k] = total
    grad = sums[0]

    squares = jnp.sum(grad * grad).reshape(1, 1)
    squares = jnp.broadcast_to(squares, (1, 128))
    squares = squares + move(squares, 1, 0)
    bits = [("s", 1 << i) for i in range(n_shard.bit_length() - 1)]
    bits += [("r", 1 << i) for i in range(1, n_replica.bit_length() - 1)]
    while bits:
        stage, bits = bits[:2], bits[2:]
        combos = [[stage[0]]] if len(stage) == 1 else [[stage[0]], [stage[1]], stage]
        parts = []
        for combo in combos:
            rb = sum(b for kind, b in combo if kind == "r")
            sb = sum(b for kind, b in combo if kind == "s")
            parts.append(move(squares, rb, sb))
        for part in parts:
            squares = squares + part
    squares = squares[0, 0]

    limit = jnp.sqrt(jnp.float32(width * columns))
    clip = jnp.minimum(jnp.float32(1.0), limit / (jnp.sqrt(squares) + 1e-06))
    scaled = clip * grad
    new_moment = 0.9 * moment + 0.1 * scaled
    new_variance = 0.95 * variance + 0.05 * scaled * scaled
    first = new_moment / (1.0 - 0.9**STEP)
    second = new_variance / (1.0 - 0.95**STEP)
    new_weight = weight - 0.01 * (first / (jnp.sqrt(second) + 1e-08) + 0.1 * weight)
    return (new_weight, new_moment, new_variance)


def solution(mesh):
    spec = P(("replica", "shard"), None)
    return jax.shard_map(shards, mesh=mesh, in_specs=(spec,) * 5, out_specs=(spec,) * 3, check_vma=False)
```

```python
import functools
import jax
import jax.numpy as jnp
from jax import lax
from jax.experimental import pallas as pl
from jax.experimental.pallas import tpu as pltpu
from jax.sharding import PartitionSpec as P

STEP = 10
AXES = ("replica", "shard")
F32 = jnp.float32
BF16 = jnp.bfloat16
VMEM = pl.BlockSpec(memory_space=pltpu.VMEM)
PARAMS = pltpu.CompilerParams(vmem_limit_bytes=32 * 2**20)
OUTER = ((0, 1), (3, 2))
INNER = ((1, 2), (2, 1))
PAIRS = ((0, 1), (1, 0), (2, 3), (3, 2))

STEPS = (
    "bx", "bc", "own0", "px0", "px1", "br0", "br1", "pr0", "kk0", "yy0", "px2", "pr1", "own1", "kk1", "rr0",
    "za0", "yy1", "px3", "pr2", "kk2", "rr1", "za1", "zb1", "yy2", "px4", "pr3", "kk3", "rr2", "za2", "zb2",
    "yy3", "pr4", "kk4", "rr3",
)
GATES = {"pr0": ("own0",)}
EXTRA = {"kk4": ("zb2",)}
COST = {"add3": 1120000000, "kk1": 280000000, "kk2": 840000000, "kk3": 1680000000, "kk4": 2800000000}
CUT = 2
LINE = {
    "za0": ("rr0", OUTER),
    "za1": ("rr1", OUTER),
    "zb1": ("rr1", INNER),
    "za2": ("rr2", PAIRS),
    "zb2": ("rr0", INNER),
}
ARRIVES = {0: (), 1: ("za0",), 2: ("zb1",), 3: ("za2", "zb2")}


def steps_for(chunks):
    names = ["bx", "bc", "own0", "own1", "br0", "br1"]
    for i in range(chunks + 1):
        names += [kind + str(i) for kind in ("px", "pr", "kk")]
        if i < chunks:
            names.append("yy%d" % i)
        if i > 0:
            names.append("rr%d" % (i - 1))
        if 0 < i < chunks:
            names.append("za%d" % (i - 1))
    return names


def flip(values, n_replica, n_shard, replica_bits, shard_bits):
    pairs = []
    for rep in range(n_replica):
        for sh in range(n_shard):
            there = (rep ^ replica_bits) * n_shard + (sh ^ shard_bits)
            pairs.append((rep * n_shard + sh, there))
    return lax.ppermute(values, AXES, pairs)


def along(values, n_shard, hops):
    size = 4 * n_shard
    pairs = [(here * size + low, there * size + low) for here, there in hops for low in range(size)]
    return lax.ppermute(values, AXES, pairs)


def gated(values, gates):
    return lax.optimization_barrier((tuple(values), tuple(gates)))[0]


def pack_kernel(chunks, n_shard, own, where, normed, *refs):
    n_out = 3 + chunks
    outs, (buf, turned, sems) = refs[:n_out], refs[n_out:]
    mine, core, cross = outs[0], outs[1], outs[2:]
    rest, x, c, y = where[0], where[1], where[2], where[3]
    width = n_shard * own
    order = [(step, 1, dc) for step in range(chunks) for dc in (0, 1)]
    order += [(step, 0, dc) for step in range(chunks) for dc in (1, 0)]
    copies = []
    for at, (step, dx, dc) in enumerate(order):
        k = chunks - 1 - step
        block = ((rest ^ k) * 2 + (x ^ dx)) * 2 + (c ^ dc)
        start = pl.multiple_of(block * width, width)
        copy = pltpu.make_async_copy(normed.at[:, pl.ds(start, width)], buf.at[at], sems.at[at])
        copy.start()
        copies.append(copy)
    for at, (step, dx, dc) in enumerate(order):
        copies[at].wait()
        turned[...] = buf[at].T
        for j in range(n_shard):
            rows = turned[pl.ds(pl.multiple_of((y ^ j) * own, own), own), :]
            if not dx:
                into = core if dc else mine
                at_row = step * width + ((j - 1) * own if j else width - own)
            elif j == 0:
                into = cross[step + 1]
                at_row = dc * (width if step + 1 < chunks else own)
            else:
                into = cross[step]
                head = own if step > 0 else 0
                at_row = dc * (head + width - own) + head + (j - 1) * own
            into[pl.ds(at_row, own), :] = rows


def pack(where, normed, chunks, n_shard, own):
    depth, group = normed.shape[0], n_shard * own
    shapes = [jax.ShapeDtypeStruct((chunks * group, depth), BF16)] * 2
    for piece in range(chunks + 1):
        rows = (own if piece > 0 else 0) + (group - own if piece < chunks else 0)
        shapes.append(jax.ShapeDtypeStruct((2 * rows, depth), BF16))
    return pl.pallas_call(
        functools.partial(pack_kernel, chunks, n_shard, own),
        out_shape=shapes,
        in_specs=[pl.BlockSpec(memory_space=pltpu.SMEM), pl.BlockSpec(memory_space=pl.ANY)],
        out_specs=[VMEM] * len(shapes),
        scratch_shapes=[
            pltpu.VMEM((4 * chunks, depth, group), BF16),
            pltpu.VMEM((group, depth), BF16),
            pltpu.SemaphoreType.DMA((4 * chunks,)),
        ],
        compiler_params=PARAMS,
        cost_estimate=pl.CostEstimate(flops=0, bytes_accessed=2 * normed.size * 2, transcendentals=0),
    )(where, normed)


def product_kernel(offset, core_offset, stay, leave, own_a, core_a, x_a, xc_a, b0, b1, b2, b3, b4, *refs):
    n_out = (stay > 0) + (leave > 0)
    extra, outs = refs[: len(refs) - n_out], refs[len(refs) - n_out :]
    cut = b3.shape[1]
    tile = 256
    work = []
    if leave:
        work.append((stay, leave, outs[0], ()))
    if stay:
        work.append((0, stay, outs[-1], extra))
    for first, rows, out, more in work:
        lhs = [own_a[pl.ds(offset + first, rows), :], core_a[pl.ds(core_offset + first, rows), :]]
        lhs += [r[pl.ds(first, rows), :] for r in (x_a, xc_a)]
        for col in range(0, out.shape[1], tile):
            last = b3[:, pl.ds(col, tile)] if col < cut else b4[:, pl.ds(col - cut, tile)]
            rhs = [r[:, pl.ds(col, tile)] for r in (b0, b1, b2)] + [last]
            total = None
            for a, b in zip(lhs, rhs):
                part = jnp.dot(a, b, preferred_element_type=F32)
                part = part.astype(BF16).astype(F32)
                total = part if total is None else total + part
            for ref in more:
                total = total + ref[:, pl.ds(col, tile)].astype(F32)
            out[:, pl.ds(col, tile)] = total.astype(out.dtype)


def product(offset, core_offset, stay, leave, lhs, rhs, extra, cost):
    columns = rhs[0].shape[1]
    shapes = [jax.ShapeDtypeStruct((leave, columns), BF16)] * (leave > 0)
    shapes += [jax.ShapeDtypeStruct((stay, columns), F32)] * (stay > 0)
    return pl.pallas_call(
        functools.partial(product_kernel, offset, core_offset, stay, leave),
        out_shape=shapes,
        in_specs=[VMEM] * (9 + len(extra)),
        out_specs=[VMEM] * len(shapes),
        compiler_params=PARAMS,
        cost_estimate=pl.CostEstimate(flops=cost, bytes_accessed=0, transcendentals=0),
    )(*lhs, *rhs, *extra)


def add_kernel(a, b, out):
    out[...] = a[...] + b[...].astype(F32)


def add(a, b, cost):
    return pl.pallas_call(
        add_kernel,
        out_shape=jax.ShapeDtypeStruct(a.shape, F32),
        in_specs=[VMEM] * 2,
        out_specs=VMEM,
        compiler_params=PARAMS,
        cost_estimate=pl.CostEstimate(flops=cost, bytes_accessed=0, transcendentals=0),
    )(a, b)


def finish_kernel(*refs):
    terms, grad, squares = refs[:-2], refs[-2], refs[-1]
    block = min(grad.shape[0], 32)
    acc = jnp.zeros((8, grad.shape[1]), F32)
    for row in range(0, grad.shape[0], block):
        total = terms[0][pl.ds(row, block), :]
        for term in terms[1:]:
            total = total + term[pl.ds(row, block), :].astype(F32)
        grad[pl.ds(row, block), :] = total
        total = total * total
        for first in range(0, block, 8):
            acc = acc + total[first : first + 8, :]
    acc = jnp.sum(acc, axis=0, keepdims=True)
    part = acc[:, :128]
    for col in range(128, grad.shape[1], 128):
        part = part + acc[:, col : col + 128]
    squares[...] = jnp.broadcast_to(part[None], squares.shape)


def finish(terms, devices):
    return pl.pallas_call(
        finish_kernel,
        out_shape=[jax.ShapeDtypeStruct(terms[0].shape, F32), jax.ShapeDtypeStruct((devices, 1, 128), F32)],
        in_specs=[VMEM] * len(terms),
        out_specs=[VMEM] * 2,
        compiler_params=PARAMS,
    )(*terms)


def update_kernel(limit, block, squares, grad, weight, moment, variance, new_weight, new_moment, new_variance):
    clip = jnp.minimum(jnp.float32(1.0), limit / (jnp.sqrt(jnp.sum(squares[...])) + 1e-06))
    rows = pl.ds(pl.multiple_of(pl.program_id(0) * block, block), block)
    scaled = clip * grad[rows, :]
    first = 0.9 * moment[rows, :] + 0.1 * scaled
    second = 0.95 * variance[rows, :] + 0.05 * scaled * scaled
    new_moment[...] = first
    new_variance[...] = second
    first = first / (1.0 - 0.9**STEP)
    second = second / (1.0 - 0.95**STEP)
    old = weight[rows, :]
    new_weight[...] = old - 0.01 * (first / (jnp.sqrt(second) + 1e-08) + 0.1 * old)


def update(squares, grad, weight, moment, variance):
    rows, columns = grad.shape
    block = min(rows, 64)
    limit = float(rows * columns * squares.shape[0]) ** 0.5
    return pl.pallas_call(
        functools.partial(update_kernel, limit, block),
        grid=(rows // block,),
        out_shape=[jax.ShapeDtypeStruct(grad.shape, F32)] * 3,
        in_specs=[VMEM] * 5,
        out_specs=[pl.BlockSpec((block, columns), lambda i: (i, 0))] * 3,
        compiler_params=PARAMS,
    )(squares, grad, weight, moment, variance)


def shards(normed, out_grads, weight, moment, variance):
    width = normed.shape[1]
    columns = out_grads.shape[1]
    n_replica = lax.axis_size("replica")
    n_shard = lax.axis_size("shard")
    chunks = n_replica // 4
    line = chunks == 4
    own = width // (n_replica * n_shard)
    group = n_shard * own
    half = columns // 2
    middle = CUT * group - own
    rep = lax.axis_index("replica")
    where = jnp.stack([rep // 4, (rep // 2) % 2, rep % 2, lax.axis_index("shard")]).astype(jnp.int32)
    packed = pack(where, normed, chunks, n_shard, own)
    a_own, a_core, cross = packed[0], packed[1], packed[2:]

    done, arriving, sums, terms = {}, [[] for _ in range(chunks)], {}, []

    def ready(name, values):
        gates = [v for gate in GATES.get(name, ()) for v in done[gate]] if line else []
        return gated(values, gates) if gates else tuple(values)

    def go(name, value, replica_bits, shard_bits):
        with jax.named_scope("mv_" + name):
            return [flip(ready(name, [value])[0], n_replica, n_shard, replica_bits, shard_bits)]

    for name in STEPS if line else steps_for(chunks):
        kind = name.rstrip("0123456789")
        step = int(name[len(kind) :] or 0)
        cost = COST.get(name, 0)
        if kind == "bx":
            out = go(name, out_grads, 2, 0)
        elif kind == "bc":
            out = go(name, out_grads, 1, 0)
        elif kind == "br":
            value = done["bx"][0]
            out = go(name, value[:, :half] if step == 0 else value[:, half:], 1, 0)
        elif kind == "own":
            out = go(name, a_core[:middle] if step == 0 else a_core[middle:], 1, 0)
        elif kind == "px":
            out = go(name, cross[step], 2, 0)
        elif kind == "pr":
            value = done["px%d" % step][0]
            out = go(name, value[value.shape[0] // 2 :], 1, 0)
        elif kind == "kk":
            stay = own if step > 0 else 0
            leave = group - own if step < chunks else 0
            offset = step * group - stay
            late = step >= CUT
            core_part = done["own1" if late else "own0"][0]
            lhs = ready(name, (a_own, core_part, done["px%d" % step][0], done["pr%d" % step][0]))
            rhs = [out_grads] + [done[b][0] for b in ("bc", "bx", "br0", "br1")]
            extra = [done[k][0] for k in EXTRA.get(name, ())] if line else []
            out = product(offset, offset - middle * late, stay, leave, lhs, rhs, extra, cost)
        elif kind == "yy":
            value = done["kk%d" % step][0]
            out = []
            for j in range(1, n_shard):
                out += go(name, value[(j - 1) * own : j * own], 0, j)
        elif kind == "rr":
            terms = [done["kk%d" % (step + 1)][-1]]
            if line and "add%d" % step in COST:
                terms = [add(terms[0], done["yy%d" % step][0], COST["add%d" % step])]
            else:
                terms += done["yy%d" % step]
            if line:
                taken = EXTRA.get("kk%d" % (step + 1), ())
                terms += [done[k][0] for k in ARRIVES[step] if k not in taken]
            else:
                terms += arriving[chunks - 1 - step]
            if step < chunks - 1:
                total = terms[0]
                for term in terms[1:]:
                    total = total + term.astype(F32)
                sums[step] = total
                out = [total.astype(BF16)]
        elif line:
            source, hops = LINE[name]
            value = done[source][0]
            if name == "zb2":
                value = (sums[0] + done["za1"][0].astype(F32)).astype(BF16)
            with jax.named_scope("mv_" + name):
                out = [along(ready(name, [value])[0], n_shard, hops)]
        else:
            k = chunks - 1 - step
            low = k & -k
            out = go(name, done["rr%d" % step][0], 4 * low, 0)
            arriving[k ^ low] += out
        done[name] = out

    grad, squares = finish(terms, n_replica * n_shard)
    with jax.named_scope("squares"):
        squares = lax.all_to_all(squares, AXES, 0, 0)
    return update(squares, grad, weight, moment, variance)


def solution(mesh):
    spec = P(AXES, None)
    return jax.shard_map(shards, mesh=mesh, in_specs=(spec,) * 5, out_specs=(spec,) * 3, check_vma=False)
```

```python
import functools
import jax
import jax.numpy as jnp
from jax import lax
from jax.experimental import pallas as pl
from jax.experimental.pallas import tpu as pltpu
from jax.sharding import PartitionSpec as P

STEP = 10
AXES = ("replica", "shard")
F32 = jnp.float32
BF16 = jnp.bfloat16
VMEM = pl.BlockSpec(memory_space=pltpu.VMEM)
PARAMS = pltpu.CompilerParams(vmem_limit_bytes=32 * 2**20)
OUTER = ((0, 1), (3, 2))
INNER = ((1, 2), (2, 1))
PAIRS = ((0, 1), (1, 0), (2, 3), (3, 2))

STEPS = (
    "bx", "bc", "own0", "px0", "px1", "br0", "br1", "pr0", "kk0", "yy0", "px2", "pr1", "own1", "kk1", "rr0",
    "za0", "yy1", "px3", "pr2", "kk2", "rr1", "za1", "zb1", "yy2", "px4", "pr3", "kk3", "rr2", "za2", "zb2",
    "yy3", "pr4", "kk4", "rr3",
)
GATES = {"px1": ("own0",)}
EXTRA = {}
COST = {"add2": 560000000, "add3": 1680000000, "fin": 224000000, "kk4": 1959999999}
CUT = 2
SPARE = 16
LINE = {
    "za0": ("rr0", OUTER),
    "za1": ("rr1", OUTER),
    "zb1": ("rr1", INNER),
    "za2": ("rr2", PAIRS),
    "zb2": ("rr0", INNER),
}
ARRIVES = {0: (), 1: ("za0",), 2: ("zb1",), 3: ("za2", "zb2")}


def steps_for(chunks):
    names = ["bx", "bc", "own0", "own1", "br0", "br1"]
    for i in range(chunks + 1):
        names += [kind + str(i) for kind in ("px", "pr", "kk")]
        if i < chunks:
            names.append("yy%d" % i)
        if i > 0:
            names.append("rr%d" % (i - 1))
        if 0 < i < chunks:
            names.append("za%d" % (i - 1))
    return names


def flip(values, n_replica, n_shard, replica_bits, shard_bits):
    pairs = []
    for rep in range(n_replica):
        for sh in range(n_shard):
            there = (rep ^ replica_bits) * n_shard + (sh ^ shard_bits)
            pairs.append((rep * n_shard + sh, there))
    return lax.ppermute(values, AXES, pairs)


def along(values, n_shard, hops):
    size = 4 * n_shard
    pairs = [(here * size + low, there * size + low) for here, there in hops for low in range(size)]
    return lax.ppermute(values, AXES, pairs)


def gated(values, gates):
    return lax.optimization_barrier((tuple(values), tuple(gates)))[0]


def pack_kernel(chunks, n_shard, own, where, normed, *refs):
    n_out = 3 + chunks
    outs, (buf, turned, sems) = refs[:n_out], refs[n_out:]
    mine, core, cross = outs[0], outs[1], outs[2:]
    rest, x, c, y = where[0], where[1], where[2], where[3]
    width = n_shard * own
    order = [(step, 1, dc) for step in range(chunks) for dc in (0, 1)]
    order += [(step, 0, dc) for step in range(chunks) for dc in (1, 0)]
    copies = []
    for at, (step, dx, dc) in enumerate(order):
        k = chunks - 1 - step
        block = ((rest ^ k) * 2 + (x ^ dx)) * 2 + (c ^ dc)
        start = pl.multiple_of(block * width, width)
        copy = pltpu.make_async_copy(normed.at[:, pl.ds(start, width)], buf.at[at], sems.at[at])
        copy.start()
        copies.append(copy)
    for at, (step, dx, dc) in enumerate(order):
        copies[at].wait()
        turned[...] = buf[at].T
        for j in range(n_shard):
            rows = turned[pl.ds(pl.multiple_of((y ^ j) * own, own), own), :]
            if not dx:
                into = core if dc else mine
                at_row = step * width + ((j - 1) * own if j else width - own)
            elif j == 0:
                into = cross[step + 1]
                at_row = dc * (width if step + 1 < chunks else own)
            else:
                into = cross[step]
                head = own if step > 0 else 0
                at_row = dc * (head + width - own) + head + (j - 1) * own
            into[pl.ds(at_row, own), :] = rows


def pack(where, normed, chunks, n_shard, own):
    depth, group = normed.shape[0], n_shard * own
    shapes = [jax.ShapeDtypeStruct((chunks * group, depth), BF16)] * 2
    for piece in range(chunks + 1):
        rows = (own if piece > 0 else 0) + (group - own if piece < chunks else 0)
        shapes.append(jax.ShapeDtypeStruct((2 * rows, depth), BF16))
    return pl.pallas_call(
        functools.partial(pack_kernel, chunks, n_shard, own),
        out_shape=shapes,
        in_specs=[pl.BlockSpec(memory_space=pltpu.SMEM), pl.BlockSpec(memory_space=pl.ANY)],
        out_specs=[VMEM] * len(shapes),
        scratch_shapes=[
            pltpu.VMEM((4 * chunks, depth, group), BF16),
            pltpu.VMEM((group, depth), BF16),
            pltpu.SemaphoreType.DMA((4 * chunks,)),
        ],
        compiler_params=PARAMS,
        cost_estimate=pl.CostEstimate(flops=0, bytes_accessed=2 * normed.size * 2, transcendentals=0),
    )(where, normed)


def product_kernel(offset, core_offset, stay, leave, own_a, core_a, x_a, xc_a, b0, b1, b2, b3, b4, *refs):
    n_out = (stay > 0) + (leave > 0)
    extra, outs = refs[: len(refs) - n_out], refs[len(refs) - n_out :]
    cut = b3.shape[1]
    tile = 256
    work = []
    if leave:
        work.append((stay, leave, outs[0], ()))
    if stay:
        work.append((0, stay, outs[-1], extra))
    for first, rows, out, more in work:
        lhs = [own_a[pl.ds(offset + first, rows), :], core_a[pl.ds(core_offset + first, rows), :]]
        lhs += [r[pl.ds(first, rows), :] for r in (x_a, xc_a)]
        for col in range(0, out.shape[1], tile):
            last = b3[:, pl.ds(col, tile)] if col < cut else b4[:, pl.ds(col - cut, tile)]
            rhs = [r[:, pl.ds(col, tile)] for r in (b0, b1, b2)] + [last]
            total = None
            for a, b in zip(lhs, rhs):
                part = jnp.dot(a, b, preferred_element_type=F32)
                part = part.astype(BF16).astype(F32)
                total = part if total is None else total + part
            for ref in more:
                total = total + ref[:, pl.ds(col, tile)].astype(F32)
            out[:, pl.ds(col, tile)] = total.astype(out.dtype)


def product(offset, core_offset, stay, leave, lhs, rhs, extra, cost):
    columns = rhs[0].shape[1]
    shapes = [jax.ShapeDtypeStruct((leave, columns), BF16)] * (leave > 0)
    shapes += [jax.ShapeDtypeStruct((stay, columns), F32)] * (stay > 0)
    return pl.pallas_call(
        functools.partial(product_kernel, offset, core_offset, stay, leave),
        out_shape=shapes,
        in_specs=[VMEM] * (9 + len(extra)),
        out_specs=[VMEM] * len(shapes),
        compiler_params=PARAMS,
        cost_estimate=pl.CostEstimate(flops=cost, bytes_accessed=0, transcendentals=0),
    )(*lhs, *rhs, *extra)


def combine_kernel(*refs):
    terms, out = refs[:-1], refs[-1]
    rows, columns = terms[0].shape
    total = terms[0][...]
    for term in terms[1:]:
        total = total + term[pl.ds(0, rows), :].astype(F32)
    out[pl.ds(0, rows), :] = total.astype(out.dtype)
    if out.shape[0] > rows:
        out[pl.ds(rows, out.shape[0] - rows), :] = jnp.zeros((out.shape[0] - rows, columns), out.dtype)


def combine(terms, dtype, cost, spare=0):
    rows, columns = terms[0].shape
    return pl.pallas_call(
        combine_kernel,
        out_shape=jax.ShapeDtypeStruct((rows + spare, columns), dtype),
        in_specs=[VMEM] * len(terms),
        out_specs=VMEM,
        compiler_params=PARAMS,
        cost_estimate=pl.CostEstimate(flops=cost, bytes_accessed=0, transcendentals=0),
    )(*terms)


def finish_kernel(*refs):
    terms, grad, squares = refs[:-2], refs[-2], refs[-1]
    block = min(grad.shape[0], 32)
    acc = jnp.zeros((8, grad.shape[1]), F32)
    for row in range(0, grad.shape[0], block):
        total = terms[0][pl.ds(row, block), :]
        for term in terms[1:]:
            total = total + term[pl.ds(row, block), :].astype(F32)
        grad[pl.ds(row, block), :] = total
        total = total * total
        for first in range(0, block, 8):
            acc = acc + total[first : first + 8, :]
    acc = jnp.sum(acc, axis=0, keepdims=True)
    part = acc[:, :128]
    for col in range(128, grad.shape[1], 128):
        part = part + acc[:, col : col + 128]
    squares[...] = jnp.broadcast_to(part[None], squares.shape)


def finish(terms, devices):
    return pl.pallas_call(
        finish_kernel,
        out_shape=[jax.ShapeDtypeStruct(terms[0].shape, F32), jax.ShapeDtypeStruct((devices, 1, 128), F32)],
        in_specs=[VMEM] * len(terms),
        out_specs=[VMEM] * 2,
        compiler_params=PARAMS,
        cost_estimate=pl.CostEstimate(flops=0, bytes_accessed=0, transcendentals=0),
    )(*terms)


def update_kernel(limit, block, squares, grad, weight, moment, variance, new_weight, new_moment, new_variance, clip):
    @pl.when(pl.program_id(0) == 0)
    def _():
        clip[0] = jnp.minimum(jnp.float32(1.0), limit / (jnp.sqrt(jnp.sum(squares[...])) + 1e-06))

    rows = pl.ds(pl.multiple_of(pl.program_id(0) * block, block), block)
    scaled = clip[0] * grad[rows, :]
    first = 0.9 * moment[rows, :] + 0.1 * scaled
    second = 0.95 * variance[rows, :] + 0.05 * scaled * scaled
    new_moment[...] = first
    new_variance[...] = second
    first = first * (1.0 / (1.0 - 0.9**STEP))
    second = second * (1.0 / (1.0 - 0.95**STEP))
    old = weight[rows, :]
    new_weight[...] = old - 0.01 * (first / (jnp.sqrt(second) + 1e-08) + 0.1 * old)


def update(squares, grad, weight, moment, variance):
    rows, columns = grad.shape
    block = min(rows, 128)
    limit = float(rows * columns * squares.shape[0]) ** 0.5
    return pl.pallas_call(
        functools.partial(update_kernel, limit, block),
        grid=(rows // block,),
        out_shape=[jax.ShapeDtypeStruct(grad.shape, F32)] * 3,
        in_specs=[VMEM] * 5,
        out_specs=[pl.BlockSpec((block, columns), lambda i: (i, 0))] * 3,
        scratch_shapes=[pltpu.SMEM((1,), F32)],
        compiler_params=PARAMS,
    )(squares, grad, weight, moment, variance)


def shards(normed, out_grads, weight, moment, variance):
    width = normed.shape[1]
    columns = out_grads.shape[1]
    n_replica = lax.axis_size("replica")
    n_shard = lax.axis_size("shard")
    chunks = n_replica // 4
    line = chunks == 4
    own = width // (n_replica * n_shard)
    group = n_shard * own
    half = columns // 2
    middle = CUT * group - own
    rep = lax.axis_index("replica")
    where = jnp.stack([rep // 4, (rep // 2) % 2, rep % 2, lax.axis_index("shard")]).astype(jnp.int32)
    packed = pack(where, normed, chunks, n_shard, own)
    a_own, a_core, cross = packed[0], packed[1], packed[2:]

    done, arriving, sums, terms = {}, [[] for _ in range(chunks)], {}, []

    def ready(name, values):
        gates = [v for gate in GATES.get(name, ()) for v in done[gate]] if line else []
        return gated(values, gates) if gates else tuple(values)

    def go(name, value, replica_bits, shard_bits):
        with jax.named_scope("mv_" + name):
            return [flip(ready(name, [value])[0], n_replica, n_shard, replica_bits, shard_bits)]

    for name in STEPS if line else steps_for(chunks):
        kind = name.rstrip("0123456789")
        step = int(name[len(kind) :] or 0)
        cost = COST.get(name, 0)
        if kind == "bx":
            out = go(name, out_grads, 2, 0)
        elif kind == "bc":
            out = go(name, out_grads, 1, 0)
        elif kind == "br":
            value = done["bx"][0]
            out = go(name, value[:, :half] if step == 0 else value[:, half:], 1, 0)
        elif kind == "own":
            out = go(name, a_core[:middle] if step == 0 else a_core[middle:], 1, 0)
        elif kind == "px":
            out = go(name, cross[step], 2, 0)
        elif kind == "pr":
            value = done["px%d" % step][0]
            out = go(name, value[value.shape[0] // 2 :], 1, 0)
        elif kind == "kk":
            stay = own if step > 0 else 0
            leave = group - own if step < chunks else 0
            offset = step * group - stay
            late = step >= CUT
            core_part = done["own1" if late else "own0"][0]
            lhs = ready(name, (a_own, core_part, done["px%d" % step][0], done["pr%d" % step][0]))
            rhs = [out_grads] + [done[b][0] for b in ("bc", "bx", "br0", "br1")]
            extra = [done[k][0] for k in EXTRA.get(name, ())] if line else []
            out = product(offset, offset - middle * late, stay, leave, lhs, rhs, extra, cost)
        elif kind == "yy":
            value = done["kk%d" % step][0]
            out = []
            for j in range(1, n_shard):
                out += go(name, value[(j - 1) * own : j * own], 0, j)
        elif kind == "rr":
            terms = [done["kk%d" % (step + 1)][-1]]
            if line and "add%d" % step in COST:
                terms = [combine([terms[0], done["yy%d" % step][0]], F32, COST["add%d" % step])]
            else:
                terms += done["yy%d" % step]
            sums[step] = list(terms)
            if line:
                taken = EXTRA.get("kk%d" % (step + 1), ())
                terms += [done[k][0] for k in ARRIVES[step] if k not in taken]
            else:
                terms += arriving[chunks - 1 - step]
            if line and step == chunks - 1 and "fin" in COST:
                terms = [combine(terms[:2], F32, COST["fin"])] + terms[2:]
            if step < chunks - 1:
                out = [combine(terms, BF16, cost)]
        elif line:
            source, hops = LINE[name]
            value = done[source][0]
            if name == "za1":
                value = combine(sums[1], BF16, cost, SPARE)
            if name == "zb2":
                value = combine(sums[0] + done["za1"], BF16, cost)
            with jax.named_scope("mv_" + name):
                out = [along(ready(name, [value])[0], n_shard, hops)]
        else:
            k = chunks - 1 - step
            low = k & -k
            out = go(name, done["rr%d" % step][0], 4 * low, 0)
            arriving[k ^ low] += out
        done[name] = out

    grad, squares = finish(terms, n_replica * n_shard)
    with jax.named_scope("squares"):
        squares = lax.all_to_all(squares, AXES, 0, 0)
    return update(squares, grad, weight, moment, variance)


def solution(mesh):
    spec = P(AXES, None)
    return jax.shard_map(shards, mesh=mesh, in_specs=(spec,) * 5, out_specs=(spec,) * 3, check_vma=False)
```

```python
import functools
import jax
import jax.numpy as jnp
from jax import lax
from jax.experimental import pallas as pl
from jax.experimental.pallas import tpu as pltpu
from jax.sharding import PartitionSpec as P

STEP = 10
AXES = ("replica", "shard")
F32 = jnp.float32
BF16 = jnp.bfloat16
VMEM = pl.BlockSpec(memory_space=pltpu.VMEM)
PARAMS = pltpu.CompilerParams(vmem_limit_bytes=32 * 2**20)
OUTER = ((0, 1), (3, 2))
INNER = ((1, 2), (2, 1))
PAIRS = ((0, 1), (1, 0), (2, 3), (3, 2))

STEPS = (
    "bx", "bc", "own0", "px0", "px1", "br0", "br1", "pr0", "kk0", "yy0", "px2", "pr1", "own1", "kk1", "rr0",
    "za0", "yy1", "px3", "pr2", "kk2", "rr1", "za1", "zb1", "yy2", "px4", "pr3", "kk3", "rr2", "za2", "zb2",
    "yy3", "pr4", "kk4", "rr3",
)
GATES = {"px1": ("own0",)}
EXTRA = {}
COST = {"add2": 560000000, "add3": 1120000000, "kk4": 1959999999}
CUT = 2
SPARE = 0
LINE = {
    "za0": ("rr0", OUTER),
    "za1": ("rr1", OUTER),
    "zb1": ("rr1", INNER),
    "za2": ("rr2", PAIRS),
    "zb2": ("rr0", INNER),
}
ARRIVES = {0: (), 1: ("za0",), 2: ("zb1",), 3: ("za2", "zb2")}


def steps_for(chunks):
    names = ["bx", "bc", "own0", "own1", "br0", "br1"]
    for i in range(chunks + 1):
        names += [kind + str(i) for kind in ("px", "pr", "kk")]
        if i < chunks:
            names.append("yy%d" % i)
        if i > 0:
            names.append("rr%d" % (i - 1))
        if 0 < i < chunks:
            names.append("za%d" % (i - 1))
    return names


def flip(values, n_replica, n_shard, replica_bits, shard_bits):
    pairs = []
    for rep in range(n_replica):
        for sh in range(n_shard):
            there = (rep ^ replica_bits) * n_shard + (sh ^ shard_bits)
            pairs.append((rep * n_shard + sh, there))
    return lax.ppermute(values, AXES, pairs)


def along(values, n_shard, hops):
    size = 4 * n_shard
    pairs = [(here * size + low, there * size + low) for here, there in hops for low in range(size)]
    return lax.ppermute(values, AXES, pairs)


def gated(values, gates):
    return lax.optimization_barrier((tuple(values), tuple(gates)))[0]


def pack_kernel(chunks, n_shard, own, where, normed, *refs):
    n_out = 3 + chunks
    outs, (buf, turned, sems) = refs[:n_out], refs[n_out:]
    mine, core, cross = outs[0], outs[1], outs[2:]
    rest, x, c, y = where[0], where[1], where[2], where[3]
    width = n_shard * own
    order = [(step, 1, dc) for step in range(chunks) for dc in (0, 1)]
    order += [(step, 0, dc) for step in range(chunks) for dc in (1, 0)]
    copies = []
    for at, (step, dx, dc) in enumerate(order):
        k = chunks - 1 - step
        block = ((rest ^ k) * 2 + (x ^ dx)) * 2 + (c ^ dc)
        start = pl.multiple_of(block * width, width)
        copy = pltpu.make_async_copy(normed.at[:, pl.ds(start, width)], buf.at[at], sems.at[at])
        copy.start()
        copies.append(copy)
    for at, (step, dx, dc) in enumerate(order):
        copies[at].wait()
        turned[...] = buf[at].T
        for j in range(n_shard):
            rows = turned[pl.ds(pl.multiple_of((y ^ j) * own, own), own), :]
            if not dx:
                into = core if dc else mine
                at_row = step * width + ((j - 1) * own if j else width - own)
            elif j == 0:
                into = cross[step + 1]
                at_row = dc * (width if step + 1 < chunks else own)
            else:
                into = cross[step]
                head = own if step > 0 else 0
                at_row = dc * (head + width - own) + head + (j - 1) * own
            into[pl.ds(at_row, own), :] = rows


def pack(where, normed, chunks, n_shard, own):
    depth, group = normed.shape[0], n_shard * own
    shapes = [jax.ShapeDtypeStruct((chunks * group, depth), BF16)] * 2
    for piece in range(chunks + 1):
        rows = (own if piece > 0 else 0) + (group - own if piece < chunks else 0)
        shapes.append(jax.ShapeDtypeStruct((2 * rows, depth), BF16))
    return pl.pallas_call(
        functools.partial(pack_kernel, chunks, n_shard, own),
        out_shape=shapes,
        in_specs=[pl.BlockSpec(memory_space=pltpu.SMEM), pl.BlockSpec(memory_space=pl.ANY)],
        out_specs=[VMEM] * len(shapes),
        scratch_shapes=[
            pltpu.VMEM((4 * chunks, depth, group), BF16),
            pltpu.VMEM((group, depth), BF16),
            pltpu.SemaphoreType.DMA((4 * chunks,)),
        ],
        compiler_params=PARAMS,
        cost_estimate=pl.CostEstimate(flops=0, bytes_accessed=2 * normed.size * 2, transcendentals=0),
    )(where, normed)


def product_kernel(offset, core_offset, stay, leave, own_a, core_a, x_a, xc_a, b0, b1, b2, b3, b4, *refs):
    n_out = (stay > 0) + (leave > 0)
    extra, outs = refs[: len(refs) - n_out], refs[len(refs) - n_out :]
    cut = b3.shape[1]
    tile = 256
    work = []
    if leave:
        work.append((stay, leave, outs[0], ()))
    if stay:
        work.append((0, stay, outs[-1], extra))
    for first, rows, out, more in work:
        lhs = [own_a[pl.ds(offset + first, rows), :], core_a[pl.ds(core_offset + first, rows), :]]
        lhs += [r[pl.ds(first, rows), :] for r in (x_a, xc_a)]
        for col in range(0, out.shape[1], tile):
            last = b3[:, pl.ds(col, tile)] if col < cut else b4[:, pl.ds(col - cut, tile)]
            rhs = [r[:, pl.ds(col, tile)] for r in (b0, b1, b2)] + [last]
            total = None
            for a, b in zip(lhs, rhs):
                part = jnp.dot(a, b, preferred_element_type=F32)
                part = part.astype(BF16).astype(F32)
                total = part if total is None else total + part
            for ref in more:
                total = total + ref[:, pl.ds(col, tile)].astype(F32)
            out[:, pl.ds(col, tile)] = total.astype(out.dtype)


def product(offset, core_offset, stay, leave, lhs, rhs, extra, cost):
    columns = rhs[0].shape[1]
    shapes = [jax.ShapeDtypeStruct((leave, columns), BF16)] * (leave > 0)
    shapes += [jax.ShapeDtypeStruct((stay, columns), F32)] * (stay > 0)
    return pl.pallas_call(
        functools.partial(product_kernel, offset, core_offset, stay, leave),
        out_shape=shapes,
        in_specs=[VMEM] * (9 + len(extra)),
        out_specs=[VMEM] * len(shapes),
        compiler_params=PARAMS,
        cost_estimate=pl.CostEstimate(flops=cost, bytes_accessed=0, transcendentals=0),
    )(*lhs, *rhs, *extra)


def combine_kernel(*refs):
    terms, out = refs[:-1], refs[-1]
    rows, columns = terms[0].shape
    total = terms[0][...]
    for term in terms[1:]:
        total = total + term[pl.ds(0, rows), :].astype(F32)
    out[pl.ds(0, rows), :] = total.astype(out.dtype)
    if out.shape[0] > rows:
        out[pl.ds(rows, out.shape[0] - rows), :] = jnp.zeros((out.shape[0] - rows, columns), out.dtype)


def combine(terms, dtype, cost, spare=0):
    rows, columns = terms[0].shape
    return pl.pallas_call(
        combine_kernel,
        out_shape=jax.ShapeDtypeStruct((rows + spare, columns), dtype),
        in_specs=[VMEM] * len(terms),
        out_specs=VMEM,
        compiler_params=PARAMS,
        cost_estimate=pl.CostEstimate(flops=cost, bytes_accessed=0, transcendentals=0),
    )(*terms)


def finish_kernel(*refs):
    terms, grad, squares = refs[:-2], refs[-2], refs[-1]
    block = min(grad.shape[0], 32)
    acc = jnp.zeros((8, grad.shape[1]), F32)
    for row in range(0, grad.shape[0], block):
        total = terms[0][pl.ds(row, block), :]
        for term in terms[1:]:
            total = total + term[pl.ds(row, block), :].astype(F32)
        grad[pl.ds(row, block), :] = total
        total = total * total
        for first in range(0, block, 8):
            acc = acc + total[first : first + 8, :]
    acc = jnp.sum(acc, axis=0, keepdims=True)
    part = acc[:, :128]
    for col in range(128, grad.shape[1], 128):
        part = part + acc[:, col : col + 128]
    squares[...] = jnp.broadcast_to(part[None], squares.shape)


def finish(terms, devices):
    return pl.pallas_call(
        finish_kernel,
        out_shape=[jax.ShapeDtypeStruct(terms[0].shape, F32), jax.ShapeDtypeStruct((devices, 1, 128), F32)],
        in_specs=[VMEM] * len(terms),
        out_specs=[VMEM] * 2,
        compiler_params=PARAMS,
        cost_estimate=pl.CostEstimate(flops=0, bytes_accessed=0, transcendentals=0),
    )(*terms)


def update_kernel(limit, block, squares, grad, weight, moment, variance, new_weight, new_moment, new_variance, clip):
    @pl.when(pl.program_id(0) == 0)
    def _():
        clip[0] = jnp.minimum(jnp.float32(1.0), limit / (jnp.sqrt(jnp.sum(squares[...])) + 1e-06))

    rows = pl.ds(pl.multiple_of(pl.program_id(0) * block, block), block)
    scaled = clip[0] * grad[rows, :]
    first = 0.9 * moment[rows, :] + 0.1 * scaled
    second = 0.95 * variance[rows, :] + 0.05 * scaled * scaled
    new_moment[...] = first
    new_variance[...] = second
    first = first * (1.0 / (1.0 - 0.9**STEP))
    second = second * (1.0 / (1.0 - 0.95**STEP))
    old = weight[rows, :]
    new_weight[...] = old - 0.01 * (first / (jnp.sqrt(second) + 1e-08) + 0.1 * old)


def update(squares, grad, weight, moment, variance):
    rows, columns = grad.shape
    block = min(rows, 128)
    limit = float(rows * columns * squares.shape[0]) ** 0.5
    return pl.pallas_call(
        functools.partial(update_kernel, limit, block),
        grid=(rows // block,),
        out_shape=[jax.ShapeDtypeStruct(grad.shape, F32)] * 3,
        in_specs=[VMEM] * 5,
        out_specs=[pl.BlockSpec((block, columns), lambda i: (i, 0))] * 3,
        scratch_shapes=[pltpu.SMEM((1,), F32)],
        compiler_params=PARAMS,
    )(squares, grad, weight, moment, variance)


def shards(normed, out_grads, weight, moment, variance):
    width = normed.shape[1]
    columns = out_grads.shape[1]
    n_replica = lax.axis_size("replica")
    n_shard = lax.axis_size("shard")
    chunks = n_replica // 4
    line = chunks == 4
    own = width // (n_replica * n_shard)
    group = n_shard * own
    half = columns // 2
    middle = CUT * group - own
    rep = lax.axis_index("replica")
    where = jnp.stack([rep // 4, (rep // 2) % 2, rep % 2, lax.axis_index("shard")]).astype(jnp.int32)
    packed = pack(where, normed, chunks, n_shard, own)
    a_own, a_core, cross = packed[0], packed[1], packed[2:]

    done, arriving, sums, terms = {}, [[] for _ in range(chunks)], {}, []

    def ready(name, values):
        gates = [v for gate in GATES.get(name, ()) for v in done[gate]] if line else []
        return gated(values, gates) if gates else tuple(values)

    def go(name, value, replica_bits, shard_bits):
        with jax.named_scope("mv_" + name):
            return [flip(ready(name, [value])[0], n_replica, n_shard, replica_bits, shard_bits)]

    for name in STEPS if line else steps_for(chunks):
        kind = name.rstrip("0123456789")
        step = int(name[len(kind) :] or 0)
        cost = COST.get(name, 0)
        if kind == "bx":
            out = go(name, out_grads, 2, 0)
        elif kind == "bc":
            out = go(name, out_grads, 1, 0)
        elif kind == "br":
            value = done["bx"][0]
            out = go(name, value[:, :half] if step == 0 else value[:, half:], 1, 0)
        elif kind == "own":
            out = go(name, a_core[:middle] if step == 0 else a_core[middle:], 1, 0)
        elif kind == "px":
            out = go(name, cross[step], 2, 0)
        elif kind == "pr":
            value = done["px%d" % step][0]
            out = go(name, value[value.shape[0] // 2 :], 1, 0)
        elif kind == "kk":
            stay = own if step > 0 else 0
            leave = group - own if step < chunks else 0
            offset = step * group - stay
            late = step >= CUT
            core_part = done["own1" if late else "own0"][0]
            lhs = ready(name, (a_own, core_part, done["px%d" % step][0], done["pr%d" % step][0]))
            rhs = [out_grads] + [done[b][0] for b in ("bc", "bx", "br0", "br1")]
            extra = [done[k][0] for k in EXTRA.get(name, ())] if line else []
            out = product(offset, offset - middle * late, stay, leave, lhs, rhs, extra, cost)
        elif kind == "yy":
            value = done["kk%d" % step][0]
            out = []
            for j in range(1, n_shard):
                out += go(name, value[(j - 1) * own : j * own], 0, j)
        elif kind == "rr":
            terms = [done["kk%d" % (step + 1)][-1]]
            if line and "add%d" % step in COST:
                terms = [combine([terms[0], done["yy%d" % step][0]], F32, COST["add%d" % step])]
            else:
                terms += done["yy%d" % step]
            sums[step] = list(terms)
            if line:
                taken = EXTRA.get("kk%d" % (step + 1), ())
                terms += [done[k][0] for k in ARRIVES[step] if k not in taken]
            else:
                terms += arriving[chunks - 1 - step]
            if line and step == chunks - 1 and "fin" in COST:
                terms = [combine(terms[:2], F32, COST["fin"])] + terms[2:]
            if step < chunks - 1:
                out = [combine(terms, BF16, cost)]
        elif line:
            source, hops = LINE[name]
            value = done[source][0]
            if name == "za1":
                value = combine(sums[1], BF16, cost, SPARE)
            if name == "zb2":
                value = combine(sums[0] + done["za1"], BF16, cost)
            with jax.named_scope("mv_" + name):
                out = [along(ready(name, [value])[0], n_shard, hops)]
        else:
            k = chunks - 1 - step
            low = k & -k
            out = go(name, done["rr%d" % step][0], 4 * low, 0)
            arriving[k ^ low] += out
        done[name] = out

    grad, squares = finish(terms, n_replica * n_shard)
    with jax.named_scope("squares"):
        squares = lax.all_to_all(squares, AXES, 0, 0)
    return update(squares, grad, weight, moment, variance)


def solution(mesh):
    spec = P(AXES, None)
    return jax.shard_map(shards, mesh=mesh, in_specs=(spec,) * 5, out_specs=(spec,) * 3, check_vma=False)
```

```python
import functools
import jax
import jax.numpy as jnp
from jax import lax
from jax.experimental import pallas as pl
from jax.experimental.pallas import tpu as pltpu
from jax.sharding import PartitionSpec as P

STEP = 10
AXES = ("replica", "shard")
F32 = jnp.float32
BF16 = jnp.bfloat16
VMEM = pl.BlockSpec(memory_space=pltpu.VMEM)
PARAMS = pltpu.CompilerParams(vmem_limit_bytes=32 * 2**20)
OUTER = ((0, 1), (3, 2))
INNER = ((1, 2), (2, 1))
PAIRS = ((0, 1), (1, 0), (2, 3), (3, 2))

STEPS = (
    "bx", "bc", "own0", "px0", "px1", "br0", "br1", "pr0", "kk0", "yy0", "px2", "pr1", "own1", "kk1", "rr0",
    "za0", "yy1", "px3", "pr2", "kk2", "rr1", "za1", "zb1", "yy2", "px4", "pr3", "kk3", "rr2", "za2", "zb2",
    "yy3", "pr4", "kk4", "rr3",
)
GATES = {"px1": ("own0",)}
EXTRA = {}
COST = {"add2": 560000000, "add3": 1120000000, "kk4": 1959999999}
CUT = 2
SPARE = 0
LINE = {
    "za0": ("rr0", OUTER),
    "za1": ("rr1", OUTER),
    "zb1": ("rr1", INNER),
    "za2": ("rr2", PAIRS),
    "zb2": ("rr0", INNER),
}
ARRIVES = {0: (), 1: ("za0",), 2: ("zb1",), 3: ("za2", "zb2")}


def steps_for(chunks):
    names = ["bx", "bc", "own0", "own1", "br0", "br1"]
    for i in range(chunks + 1):
        names += [kind + str(i) for kind in ("px", "pr", "kk")]
        if i < chunks:
            names.append("yy%d" % i)
        if i > 0:
            names.append("rr%d" % (i - 1))
        if 0 < i < chunks:
            names.append("za%d" % (i - 1))
    return names


def flip(values, n_replica, n_shard, replica_bits, shard_bits):
    pairs = []
    for rep in range(n_replica):
        for sh in range(n_shard):
            there = (rep ^ replica_bits) * n_shard + (sh ^ shard_bits)
            pairs.append((rep * n_shard + sh, there))
    return lax.ppermute(values, AXES, pairs)


def along(values, n_shard, hops):
    size = 4 * n_shard
    pairs = [(here * size + low, there * size + low) for here, there in hops for low in range(size)]
    return lax.ppermute(values, AXES, pairs)


def gated(values, gates):
    return lax.optimization_barrier((tuple(values), tuple(gates)))[0]


def pack_kernel(chunks, n_shard, own, where, normed, *refs):
    n_out = 3 + chunks
    outs, (buf, turned, sems) = refs[:n_out], refs[n_out:]
    mine, core, cross = outs[0], outs[1], outs[2:]
    rest, x, c, y = where[0], where[1], where[2], where[3]
    width = n_shard * own
    order = [(step, 1, dc) for step in range(chunks) for dc in (0, 1)]
    order += [(step, 0, dc) for step in range(chunks) for dc in (1, 0)]
    copies = []
    for at, (step, dx, dc) in enumerate(order):
        k = chunks - 1 - step
        block = ((rest ^ k) * 2 + (x ^ dx)) * 2 + (c ^ dc)
        start = pl.multiple_of(block * width, width)
        copy = pltpu.make_async_copy(normed.at[:, pl.ds(start, width)], buf.at[at], sems.at[at])
        copy.start()
        copies.append(copy)
    for at, (step, dx, dc) in enumerate(order):
        copies[at].wait()
        turned[...] = buf[at].T
        for j in range(n_shard):
            rows = turned[pl.ds(pl.multiple_of((y ^ j) * own, own), own), :]
            if not dx:
                into = core if dc else mine
                at_row = step * width + ((j - 1) * own if j else width - own)
            elif j == 0:
                into = cross[step + 1]
                at_row = dc * (width if step + 1 < chunks else own)
            else:
                into = cross[step]
                head = own if step > 0 else 0
                at_row = dc * (head + width - own) + head + (j - 1) * own
            into[pl.ds(at_row, own), :] = rows


def pack(where, normed, chunks, n_shard, own):
    depth, group = normed.shape[0], n_shard * own
    shapes = [jax.ShapeDtypeStruct((chunks * group, depth), BF16)] * 2
    for piece in range(chunks + 1):
        rows = (own if piece > 0 else 0) + (group - own if piece < chunks else 0)
        shapes.append(jax.ShapeDtypeStruct((2 * rows, depth), BF16))
    return pl.pallas_call(
        functools.partial(pack_kernel, chunks, n_shard, own),
        out_shape=shapes,
        in_specs=[pl.BlockSpec(memory_space=pltpu.SMEM), pl.BlockSpec(memory_space=pl.ANY)],
        out_specs=[VMEM] * len(shapes),
        scratch_shapes=[
            pltpu.VMEM((4 * chunks, depth, group), BF16),
            pltpu.VMEM((group, depth), BF16),
            pltpu.SemaphoreType.DMA((4 * chunks,)),
        ],
        compiler_params=PARAMS,
        cost_estimate=pl.CostEstimate(flops=0, bytes_accessed=2 * normed.size * 2, transcendentals=0),
    )(where, normed)


def product_kernel(offset, core_offset, stay, leave, own_a, core_a, x_a, xc_a, b0, b1, b2, b3, b4, *refs):
    n_out = (stay > 0) + (leave > 0)
    extra, outs = refs[: len(refs) - n_out], refs[len(refs) - n_out :]
    cut = b3.shape[1]
    tile = 512
    work = []
    if leave:
        work.append((stay, leave, outs[0], ()))
    if stay:
        work.append((0, stay, outs[-1], extra))
    for first, rows, out, more in work:
        lhs = [own_a[pl.ds(offset + first, rows), :], core_a[pl.ds(core_offset + first, rows), :]]
        lhs += [r[pl.ds(first, rows), :] for r in (x_a, xc_a)]
        for col in range(0, out.shape[1], tile):
            last = b3[:, pl.ds(col, tile)] if col < cut else b4[:, pl.ds(col - cut, tile)]
            rhs = [r[:, pl.ds(col, tile)] for r in (b0, b1, b2)] + [last]
            total = None
            for a, b in zip(lhs, rhs):
                part = jnp.dot(a, b, preferred_element_type=F32)
                part = part.astype(BF16).astype(F32)
                total = part if total is None else total + part
            for ref in more:
                total = total + ref[:, pl.ds(col, tile)].astype(F32)
            out[:, pl.ds(col, tile)] = total.astype(out.dtype)


def product(offset, core_offset, stay, leave, lhs, rhs, extra, cost):
    columns = rhs[0].shape[1]
    shapes = [jax.ShapeDtypeStruct((leave, columns), BF16)] * (leave > 0)
    shapes += [jax.ShapeDtypeStruct((stay, columns), F32)] * (stay > 0)
    return pl.pallas_call(
        functools.partial(product_kernel, offset, core_offset, stay, leave),
        out_shape=shapes,
        in_specs=[VMEM] * (9 + len(extra)),
        out_specs=[VMEM] * len(shapes),
        compiler_params=PARAMS,
        cost_estimate=pl.CostEstimate(flops=cost, bytes_accessed=0, transcendentals=0),
    )(*lhs, *rhs, *extra)


def combine_kernel(*refs):
    terms, out = refs[:-1], refs[-1]
    rows, columns = terms[0].shape
    total = terms[0][...]
    for term in terms[1:]:
        total = total + term[pl.ds(0, rows), :].astype(F32)
    out[pl.ds(0, rows), :] = total.astype(out.dtype)
    if out.shape[0] > rows:
        out[pl.ds(rows, out.shape[0] - rows), :] = jnp.zeros((out.shape[0] - rows, columns), out.dtype)


def combine(terms, dtype, cost, spare=0):
    rows, columns = terms[0].shape
    return pl.pallas_call(
        combine_kernel,
        out_shape=jax.ShapeDtypeStruct((rows + spare, columns), dtype),
        in_specs=[VMEM] * len(terms),
        out_specs=VMEM,
        compiler_params=PARAMS,
        cost_estimate=pl.CostEstimate(flops=cost, bytes_accessed=0, transcendentals=0),
    )(*terms)


def finish_kernel(*refs):
    terms, grad, squares = refs[:-2], refs[-2], refs[-1]
    block = min(grad.shape[0], 32)
    acc = jnp.zeros((8, grad.shape[1]), F32)
    for row in range(0, grad.shape[0], block):
        total = terms[0][pl.ds(row, block), :]
        for term in terms[1:]:
            total = total + term[pl.ds(row, block), :].astype(F32)
        grad[pl.ds(row, block), :] = total
        total = total * total
        for first in range(0, block, 8):
            acc = acc + total[first : first + 8, :]
    acc = jnp.sum(acc, axis=0, keepdims=True)
    part = acc[:, :128]
    for col in range(128, grad.shape[1], 128):
        part = part + acc[:, col : col + 128]
    squares[...] = jnp.broadcast_to(part[None], squares.shape)


def finish(terms, devices):
    return pl.pallas_call(
        finish_kernel,
        out_shape=[jax.ShapeDtypeStruct(terms[0].shape, F32), jax.ShapeDtypeStruct((devices, 1, 128), F32)],
        in_specs=[VMEM] * len(terms),
        out_specs=[VMEM] * 2,
        compiler_params=PARAMS,
        cost_estimate=pl.CostEstimate(flops=0, bytes_accessed=0, transcendentals=0),
    )(*terms)


def update_kernel(limit, block, squares, grad, weight, moment, variance, new_weight, new_moment, new_variance, clip):
    @pl.when(pl.program_id(0) == 0)
    def _():
        clip[0] = jnp.minimum(jnp.float32(1.0), limit / (jnp.sqrt(jnp.sum(squares[...])) + 1e-06))

    rows = pl.ds(pl.multiple_of(pl.program_id(0) * block, block), block)
    scaled = clip[0] * grad[rows, :]
    first = 0.9 * moment[rows, :] + 0.1 * scaled
    second = 0.95 * variance[rows, :] + 0.05 * scaled * scaled
    new_moment[...] = first
    new_variance[...] = second
    first = first * (1.0 / (1.0 - 0.9**STEP))
    second = second * (1.0 / (1.0 - 0.95**STEP))
    old = weight[rows, :]
    new_weight[...] = old - 0.01 * (first / (jnp.sqrt(second) + 1e-08) + 0.1 * old)


def update(squares, grad, weight, moment, variance):
    rows, columns = grad.shape
    block = min(rows, 128)
    limit = float(rows * columns * squares.shape[0]) ** 0.5
    return pl.pallas_call(
        functools.partial(update_kernel, limit, block),
        grid=(rows // block,),
        out_shape=[jax.ShapeDtypeStruct(grad.shape, F32)] * 3,
        in_specs=[VMEM] * 5,
        out_specs=[pl.BlockSpec((block, columns), lambda i: (i, 0))] * 3,
        scratch_shapes=[pltpu.SMEM((1,), F32)],
        compiler_params=PARAMS,
    )(squares, grad, weight, moment, variance)


def shards(normed, out_grads, weight, moment, variance):
    width = normed.shape[1]
    columns = out_grads.shape[1]
    n_replica = lax.axis_size("replica")
    n_shard = lax.axis_size("shard")
    chunks = n_replica // 4
    line = chunks == 4
    own = width // (n_replica * n_shard)
    group = n_shard * own
    half = columns // 2
    middle = CUT * group - own
    rep = lax.axis_index("replica")
    where = jnp.stack([rep // 4, (rep // 2) % 2, rep % 2, lax.axis_index("shard")]).astype(jnp.int32)
    packed = pack(where, normed, chunks, n_shard, own)
    a_own, a_core, cross = packed[0], packed[1], packed[2:]

    done, arriving, sums, terms = {}, [[] for _ in range(chunks)], {}, []

    def ready(name, values):
        gates = [v for gate in GATES.get(name, ()) for v in done[gate]] if line else []
        return gated(values, gates) if gates else tuple(values)

    def go(name, value, replica_bits, shard_bits):
        with jax.named_scope("mv_" + name):
            return [flip(ready(name, [value])[0], n_replica, n_shard, replica_bits, shard_bits)]

    for name in STEPS if line else steps_for(chunks):
        kind = name.rstrip("0123456789")
        step = int(name[len(kind) :] or 0)
        cost = COST.get(name, 0)
        if kind == "bx":
            out = go(name, out_grads, 2, 0)
        elif kind == "bc":
            out = go(name, out_grads, 1, 0)
        elif kind == "br":
            value = done["bx"][0]
            out = go(name, value[:, :half] if step == 0 else value[:, half:], 1, 0)
        elif kind == "own":
            out = go(name, a_core[:middle] if step == 0 else a_core[middle:], 1, 0)
        elif kind == "px":
            out = go(name, cross[step], 2, 0)
        elif kind == "pr":
            value = done["px%d" % step][0]
            out = go(name, value[value.shape[0] // 2 :], 1, 0)
        elif kind == "kk":
            stay = own if step > 0 else 0
            leave = group - own if step < chunks else 0
            offset = step * group - stay
            late = step >= CUT
            core_part = done["own1" if late else "own0"][0]
            lhs = ready(name, (a_own, core_part, done["px%d" % step][0], done["pr%d" % step][0]))
            rhs = [out_grads] + [done[b][0] for b in ("bc", "bx", "br0", "br1")]
            extra = [done[k][0] for k in EXTRA.get(name, ())] if line else []
            out = product(offset, offset - middle * late, stay, leave, lhs, rhs, extra, cost)
        elif kind == "yy":
            value = done["kk%d" % step][0]
            out = []
            for j in range(1, n_shard):
                out += go(name, value[(j - 1) * own : j * own], 0, j)
        elif kind == "rr":
            terms = [done["kk%d" % (step + 1)][-1]]
            if line and "add%d" % step in COST:
                terms = [combine([terms[0], done["yy%d" % step][0]], F32, COST["add%d" % step])]
            else:
                terms += done["yy%d" % step]
            sums[step] = list(terms)
            if line:
                taken = EXTRA.get("kk%d" % (step + 1), ())
                terms += [done[k][0] for k in ARRIVES[step] if k not in taken]
            else:
                terms += arriving[chunks - 1 - step]
            if line and step == chunks - 1 and "fin" in COST:
                terms = [combine(terms[:2], F32, COST["fin"])] + terms[2:]
            if step < chunks - 1:
                out = [combine(terms, BF16, cost)]
        elif line:
            source, hops = LINE[name]
            value = done[source][0]
            if name == "za1":
                value = combine(sums[1], BF16, cost, SPARE)
            if name == "zb2":
                value = combine(sums[0] + done["za1"], BF16, cost)
            with jax.named_scope("mv_" + name):
                out = [along(ready(name, [value])[0], n_shard, hops)]
        else:
            k = chunks - 1 - step
            low = k & -k
            out = go(name, done["rr%d" % step][0], 4 * low, 0)
            arriving[k ^ low] += out
        done[name] = out

    grad, squares = finish(terms, n_replica * n_shard)
    with jax.named_scope("squares"):
        squares = lax.all_to_all(squares, AXES, 0, 0)
    return update(squares, grad, weight, moment, variance)


def solution(mesh):
    spec = P(AXES, None)
    return jax.shard_map(shards, mesh=mesh, in_specs=(spec,) * 5, out_specs=(spec,) * 3, check_vma=False)
```
